32 devices in a mesh: req: 4 (over y, x), tile: 4 (over z), col: 2 (over core).
Axes of the slice: x: 2, y: 2, z: 4, core: 2. Of those that a mesh axis runs over, the one named last changes fastest.
Arguments:
- img_qkv: bfloat16 [4, 64, 64, 3, 1536], P('req', 'tile', None, None, 'col'), may hold values from -10 to 10
- txt_kv: bfloat16 [4, 512, 2, 1536], P('req', 'tile', None, 'col'), may hold values from -8 to 8
- text_len: int32 [4], P('req'), may hold values from 256 to 512, as said below
- hidden_state: bfloat16 [4, 64, 64, 3072], P('req', 'tile', 'col'), may hold values from -3 to 3
- modulation: float32 [28, 4, 3, 3072], P(None, 'req'), may hold values from 0.1 to 1.9
- w_attn_out: bfloat16 [1536, 3072], replicated, may hold values from -0.15625 to 0.15625
- w_final: bfloat16 [3072, 64], replicated, may hold values from -0.109375 to 0.109375
- latent: float32 [4, 64, 64, 64], P('req', 'tile', 'col'), may hold values from -6 to 6
- sigmas: float32 [29], replicated, may hold values from -1 to 3, as said below
- step_index: int32 [1], replicated, may hold values from 0 to 27
- w_preview: float32 [3, 3, 64, 64], replicated, may hold values from -0.25 to 0.25
Outputs:
- velocity: float32 [4, 64, 64, 64], P('req', 'tile', 'col')
- latent_next: float32 [4, 64, 64, 64], P('req', 'tile', 'col')
- preview: float32 [4, 64, 64, 64], P('req', 'tile', 'col')
The draws below stay inside these ranges and needn't reach their ends.
Inputs may be any that keep to these rules, and one draw needn't show every extreme that they name: `text_len`: some request has exactly 512 live text tokens. sigmas[i] - sigmas[i + 1] lies between 0.1 / 28 and 3.4 / 28.
All inputs are finite; a program needn't handle non-finite values.
Results may differ from the reference program's by a relative error of at most 0.005.
Values may be sent and summed in bfloat16 or wider, within the bound.
A program may use at most 320 MiB of HBM per device.

```python
import math
import jax
import jax.numpy as jnp
from jax import lax

GH = 64
GW = 64
TXT = 512
HEADS = 12
HD = 128
D = 3072
C = 64
STEPS = 28
REQS = 4


def draw_img_qkv(key, part):
    shape = (REQS, GH, GW, 3, HEADS * HD)
    scales = jnp.array([1.4, 1.4, 1.0], jnp.float32).reshape(1, 1, 1, 3, 1)
    values = jnp.clip(jax.random.normal(key, shape, jnp.float32), -6.0, 6.0) * scales
    return values.astype(jnp.bfloat16)


def draw_text_len(key, part):
    lengths = jax.random.randint(key, (REQS,), TXT // 2, TXT + 1)
    chosen = jax.random.randint(jax.random.fold_in(key, 3), (), 0, REQS)
    return jnp.where(jnp.arange(REQS) == chosen, TXT, lengths).astype(jnp.int32)


def draw_sigmas(key, part):
    steps_at = jnp.arange(STEPS + 1).astype(jnp.float32)
    amplitude = jax.random.uniform(jax.random.fold_in(key, 5), (), jnp.float32, 1.0, 2.5)
    jitter = jax.random.uniform(key, (STEPS + 1,), jnp.float32, -0.45, 0.45)
    return amplitude * (1.0 - steps_at / STEPS) + jitter / STEPS


def block_levels(rng, shape, split, low, largest):
    gain, own = 1.0, jax.random.fold_in(rng, 6)
    for dim, parts in split:
        draws = jnp.exp(jax.random.uniform(jax.random.fold_in(own, dim), (parts,), jnp.float32, low / len(split), largest / len(split)))
        gain = gain * jnp.repeat(draws, shape[dim] // parts).reshape([-1 if axis == dim else 1 for axis in range(len(shape))])
    return gain


def noise(key, extent, width, most, cuts=(), kind=jnp.bfloat16):
    drawn = width * jax.random.normal(key, extent, jnp.float32)
    if cuts:
        drawn = drawn * block_levels(key, extent, cuts, -0.22, 0.18)
    return jnp.clip(drawn, -most, most).astype(kind)


def setup_inputs(seed: int = 0) -> dict:
    arg_keys = jax.random.split(jax.random.key(seed), 12)
    img_qkv = draw_img_qkv(jax.random.fold_in(arg_keys[11], 71), 0)
    txt_kv = noise(arg_keys[1], (REQS, TXT, 2, HEADS * HD), 1.4, 8.0, ((0, 4), (1, 4), (3, 2)))
    text_len = draw_text_len(jax.random.fold_in(arg_keys[11], 71), 0)
    hidden_state = noise(arg_keys[3], (REQS, GH, GW, D), 0.3, 3.0, ((0, 4), (1, 4), (2, 2)))
    modulation = jnp.clip(1.0 + 0.18 * jax.random.normal(arg_keys[4], (STEPS, REQS, 3, D), jnp.float32), 0.1, 1.9)
    w_attn_out = noise(arg_keys[5], (HEADS * HD, D), (HEADS * HD) ** -0.5, 0.15625)
    w_final = noise(arg_keys[6], (D, C), D ** -0.5, 0.109375)
    latent = noise(arg_keys[7], (REQS, GH, GW, C), 1.0, 6.0, ((0, 4), (1, 4), (2, 2)), jnp.float32)
    sigmas = draw_sigmas(jax.random.fold_in(arg_keys[11], 71), 0)
    step_index = jax.random.randint(arg_keys[9], (1,), 0, STEPS).astype(jnp.int32)
    w_preview = noise(arg_keys[10], (3, 3, C, C), (9 * C) ** -0.5, 0.25, (), jnp.float32)
    return {"img_qkv": img_qkv, "txt_kv": txt_kv, "text_len": text_len, "hidden_state": hidden_state, "modulation": modulation, "w_attn_out": w_attn_out, "w_final": w_final, "latent": latent, "sigmas": sigmas, "step_index": step_index, "w_preview": w_preview}


norm_eps = 1e-06

def attention(queries, key_part, value_part, key_live):
    score_scale = 1.0 / math.sqrt(HD)

    def one_head(head_id):
        head_query = lax.dynamic_index_in_dim(queries, head_id, 1, keepdims=False)
        head_keys = lax.dynamic_index_in_dim(key_part, head_id, 1, keepdims=False)
        head_values = lax.dynamic_index_in_dim(value_part, head_id, 1, keepdims=False)
        scores = jnp.dot(head_query, head_keys.T, preferred_element_type=jnp.float32) * score_scale
        scores = jnp.where(key_live[None, :], scores, -jnp.inf)
        row_max = lax.optimization_barrier(jnp.max(scores, axis=1, keepdims=True))
        probs = jnp.exp(scores - row_max)
        denom = lax.optimization_barrier(jnp.sum(probs, axis=1, keepdims=True))
        summed = jnp.dot(probs.astype(jnp.bfloat16), head_values, preferred_element_type=jnp.float32)
        return summed / denom
    return lax.map(one_head, jnp.arange(HEADS, dtype=jnp.int32))

def reference(img_qkv, txt_kv, text_len, hidden_state, modulation, w_attn_out, w_final, latent, sigmas, step_index, w_preview):
    step_now = step_index[0]
    sigma_step = sigmas[step_now + 1] - sigmas[step_now]
    mod_now = lax.dynamic_index_in_dim(modulation, step_now, 0, keepdims=False)
    vel_list = []
    next_list = []
    view_list = []
    for request in range(REQS):
        img_part = img_qkv[request].reshape(GH * GW, 3, HEADS, HD)
        txt_part = txt_kv[request].reshape(TXT, 2, HEADS, HD)
        key_part = jnp.concatenate([img_part[:, 1], txt_part[:, 0]], axis=0)
        value_part = jnp.concatenate([img_part[:, 2], txt_part[:, 1]], axis=0)
        key_live = jnp.concatenate([jnp.ones((GH * GW,), bool), jnp.arange(TXT, dtype=jnp.int32) < text_len[request]])
        head_out = attention(img_part[:, 0], key_part, value_part, key_live)
        attended = jnp.transpose(head_out, (1, 0, 2)).reshape(GH * GW, HEADS * HD).astype(jnp.bfloat16)
        branch = jnp.dot(attended, w_attn_out, preferred_element_type=jnp.float32)
        mixed_state = hidden_state[request].reshape(GH * GW, D).astype(jnp.float32) + mod_now[request, 0][None, :] * branch
        row_mean = lax.optimization_barrier(jnp.mean(mixed_state, axis=1, keepdims=True))
        centred = mixed_state - row_mean
        row_var = lax.optimization_barrier(jnp.mean(centred * centred, axis=1, keepdims=True))
        normed = centred / jnp.sqrt(row_var + norm_eps) * (1.0 + mod_now[request, 2][None, :]) + mod_now[request, 1][None, :]
        normed = normed.astype(jnp.bfloat16)
        velocity = jnp.dot(normed, w_final, preferred_element_type=jnp.float32)
        updated = latent[request].reshape(GH * GW, C) + sigma_step * velocity
        grid_field = updated.reshape(GH, GW, C)
        padded = jnp.pad(grid_field, ((1, 1), (1, 1), (0, 0)))
        preview = jnp.zeros((GH, GW, C), jnp.float32)
        for row_off in range(3):
            for col_off in range(3):
                preview = preview + jnp.einsum('yxc,cd->yxd', padded[row_off:row_off + GH, col_off:col_off + GW], w_preview[row_off, col_off], precision=lax.Precision.HIGHEST)
        vel_list.append(velocity.reshape(GH, GW, C))
        next_list.append(grid_field)
        view_list.append(preview)
    return (jnp.stack(vel_list), jnp.stack(next_list), jnp.stack(view_list))
```

```python
import functools
import math

import jax
import jax.numpy as jnp
from jax import lax
from jax.experimental import pallas as pl
from jax.experimental.pallas import tpu as pltpu
from jax.sharding import PartitionSpec as P

HD = 128


norm_eps = 1e-06


def padded_2(cells, sides, width):
    for axis, dim in sides:
        count = lax.axis_size(axis)
        ends = count - 1
        head = lax.slice_in_dim(cells, 0, width, axis=dim)
        tail = lax.slice_in_dim(cells, cells.shape[dim] - width, cells.shape[dim], axis=dim)
        cells = jnp.concatenate(
            [
                lax.ppermute(tail, axis, [(i, (i + 1) % count) for i in range(ends)]),
                cells,
                lax.ppermute(head, axis, [((i + 1) % count, i) for i in range(ends)]),
            ],
            axis=dim,
        )
    return cells


def make_fold(queries, img_rows, text_rows, text_limit):
    score_scale = 1.0 / math.sqrt(HD)
    shard_rows = img_rows + text_rows

    def fold_step(carry, piece, start):
        run_max, run_sum, run_acc = carry
        piece_len = piece.shape[0]
        key_index = jnp.arange(piece_len, dtype=jnp.int32)
        in_shard = key_index % shard_rows
        text_pos = key_index // shard_rows * text_rows + in_shard - img_rows
        key_live = (in_shard < img_rows) | (text_pos < text_limit)
        scores = (
            jnp.einsum("qhd,khd->hqk", queries, piece[:, 0], preferred_element_type=jnp.float32)
            * score_scale
        )
        scores = jnp.where(key_live[None, None, :], scores, -1e30)
        new_max = jnp.maximum(run_max, jnp.max(scores, axis=2))
        weights = jnp.where(key_live[None, None, :], jnp.exp(scores - new_max[:, :, None]), 0.0)
        run_sum = jnp.sum(weights, axis=2)
        run_acc = jnp.einsum(
            "hqk,khd->hqd",
            weights.astype(jnp.bfloat16),
            piece[:, 1],
            preferred_element_type=jnp.float32,
        )
        return (new_max, run_sum, run_acc)

    return fold_step


def start_carry(query_rows, head_count):
    return (
        jnp.full((head_count, query_rows), -1e30, jnp.float32),
        jnp.zeros((head_count, query_rows), jnp.float32),
        jnp.zeros((head_count, query_rows, HD), jnp.float32),
    )


def finish(carry):
    run_max, run_sum, run_acc = carry
    return jnp.transpose(run_acc / run_sum[:, :, None], (1, 0, 2)).astype(jnp.bfloat16)


def attend_kernel(moves, key_chunk, image_keys, q_ref, bias_ref, *refs):
    parts = refs[:-3]
    o_ref, kbuf, vbuf = refs[-3:]

    @pl.when(pl.program_id(0) == 0)
    def _():
        vbuf[:, HD:] = jnp.ones((vbuf.shape[0], HD), jnp.bfloat16)
        for which, block, k_from, v_from, size, to in moves:
            kbuf[to : to + size, :] = parts[which][block, k_from : k_from + size, :]
            vbuf[to : to + size, :HD] = parts[which][block, v_from : v_from + size, :]

    factor = math.log2(math.e) / math.sqrt(HD)
    queries = q_ref[0]
    all_keys = kbuf.shape[0]
    pieces = [(at, key_chunk) for at in range(0, image_keys, key_chunk)]
    pieces.append((image_keys, all_keys - image_keys))
    run_max = acc = None
    for at, size in pieces:
        scores = (
            lax.dot_general(
                queries,
                kbuf[at : at + size, :],
                (((1,), (1,)), ((), ())),
                preferred_element_type=jnp.float32,
            )
            * factor
        )
        if at == image_keys:
            scores = scores + bias_ref[...]
        top = jnp.max(scores, axis=1, keepdims=True)
        new_max = top if run_max is None else jnp.maximum(run_max, top)
        probs = jnp.exp2(scores - new_max).astype(jnp.bfloat16)
        term = jnp.dot(probs, vbuf[at : at + size, :], preferred_element_type=jnp.float32)
        acc = term if acc is None else acc * jnp.exp2(run_max - new_max) + term
        run_max = new_max
    o_ref[0] = (acc[:, :HD] / acc[:, HD:]).astype(jnp.bfloat16)


def attend(block, others, bias, query_rows, moves, image_keys, q_tile, key_chunk):
    blocks = block.shape[0]
    per_block = query_rows // q_tile
    all_keys = image_keys + bias.shape[1]
    parts = (block,) + others

    def whole(array):
        return pl.BlockSpec(array.shape, lambda i: (0,) * array.ndim)

    queries = blocks * query_rows
    return pl.pallas_call(
        functools.partial(attend_kernel, moves, key_chunk, image_keys),
        grid=(blocks * per_block,),
        out_shape=jax.ShapeDtypeStruct((blocks, query_rows, HD), jnp.bfloat16),
        in_specs=[
            pl.BlockSpec((1, q_tile, HD), lambda i: (i // per_block, i % per_block, 0)),
            whole(bias),
        ]
        + [whole(part) for part in parts],
        out_specs=pl.BlockSpec((1, q_tile, HD), lambda i: (i // per_block, i % per_block, 0)),
        scratch_shapes=[
            pltpu.VMEM((all_keys, HD), jnp.bfloat16),
            pltpu.VMEM((all_keys, 2 * HD), jnp.bfloat16),
        ],
        compiler_params=pltpu.CompilerParams(vmem_limit_bytes=48 * 1024 * 1024),
        cost_estimate=pl.CostEstimate(
            flops=6 * queries * all_keys * HD,
            bytes_accessed=2 * sum(part.size for part in parts) + 4 * queries * HD,
            transcendentals=queries * all_keys,
        ),
    )(block, bias, *parts)


def tile_mixed(cells):
    return lax.all_to_all(cells, "tile", split_axis=0, concat_axis=0, tiled=True)


def by_heads(img_qkv, txt_kv, text_limit, tile_cols):
    rows, grid_cols = img_qkv.shape[1:3]
    heads = img_qkv.shape[4] // HD
    text_rows = txt_kv.shape[1]
    tiles = lax.axis_size("tile")
    halves = grid_cols // tile_cols
    own = rows * tile_cols
    full = own * halves
    text_half = text_rows // halves
    me = lax.axis_index("col")

    img = jnp.transpose(
        img_qkv[0].reshape(rows, halves, tile_cols, 3, heads, HD), (4, 3, 1, 0, 2, 5)
    ).reshape(heads, 3, halves, own, HD)
    txt = jnp.transpose(txt_kv[0].reshape(text_rows, 2, heads, HD), (2, 1, 0, 3))

    img_a = img[:tiles].reshape(tiles, 3, full, HD)
    txt_a = txt[:tiles]
    send_a = jnp.concatenate(
        [img_a[:, 0], img_a[:, 1], txt_a[:, 0], img_a[:, 2], txt_a[:, 1]], axis=1
    )
    got_a = tile_mixed(send_a)

    img_b = img[tiles:]
    txt_b = txt[tiles:].reshape(heads - tiles, 2, halves, text_half, HD)
    send_b = jnp.stack(
        [
            jnp.concatenate(
                [
                    img_b[:, 0, half],
                    img_b[:, 1, half],
                    txt_b[:, 0, half],
                    img_b[:, 2, half],
                    txt_b[:, 1, half],
                ],
                axis=1,
            )
            for half in range(halves)
        ]
    )
    mixed_b = lax.all_to_all(send_b, "col", split_axis=0, concat_axis=0, tiled=True)
    got_b = tile_mixed(mixed_b.reshape(tiles, send_b.shape[2], HD))
    other_b = lax.ppermute(got_b[:, own:], "col", [(0, 1), (1, 0)])

    text_all = tiles * text_rows
    image_all = tiles * full
    place = jnp.arange(text_all, dtype=jnp.int32)
    bias_a = jnp.where(place < text_limit, 0.0, -1e30).astype(jnp.float32)[None]
    side, within = place // (tiles * text_half), place % (tiles * text_half)
    place_b = (
        within // text_half * text_rows
        + jnp.where(side == 0, me, 1 - me) * text_half
        + within % text_half
    )
    bias_b = jnp.where(place_b < text_limit, 0.0, -1e30).astype(jnp.float32)[None]

    moves_a, moves_b = [], []
    for t in range(tiles):
        key, value = full, 2 * full + text_rows
        moves_a.append((0, t, key, value, full, t * full))
        moves_a.append((0, t, key + full, value + full, text_rows, image_all + t * text_rows))
    for s in range(halves):
        for t in range(tiles):
            key = own if s == 0 else 0
            value = key + own + text_half
            slot = s * tiles + t
            moves_b.append((s, t, key, value, own, slot * own))
            moves_b.append(
                (s, t, key + own, value + own, text_half, image_all + slot * text_half)
            )
    out_a = tile_mixed(attend(got_a, (), bias_a, full, tuple(moves_a), image_all, 512, 1024))
    out_b = tile_mixed(
        attend(got_b, (other_b,), bias_b, own, tuple(moves_b), image_all, 512, 1024)
    )
    out_a = jnp.transpose(out_a.reshape(tiles, halves, own, HD), (1, 0, 2, 3))
    out_a = lax.all_to_all(out_a, "col", split_axis=0, concat_axis=0, tiled=True)
    every = jnp.concatenate([out_a.reshape(halves * tiles, own, HD), out_b], axis=0)
    order = [c * heads + t for c in range(halves) for t in range(tiles)]
    order += [c * heads + h for c in range(halves) for h in range(tiles, heads)]
    return every, order


def body(
    img_qkv,
    txt_kv,
    text_len,
    hidden_state,
    modulation,
    w_attn_out,
    w_final,
    latent,
    sigmas,
    step_index,
    w_preview,
):
    tile_rows = img_qkv.shape[1]
    grid_cols = img_qkv.shape[2]
    local_heads = img_qkv.shape[4] // HD
    text_rows = txt_kv.shape[1]
    tile_cols = hidden_state.shape[2]
    col_count = grid_cols // tile_cols
    own_rows = tile_rows * tile_cols
    text_limit = text_len[0]
    all_heads = local_heads * col_count
    tiles = lax.axis_size("tile")
    if col_count == 2 and (local_heads - tiles) * col_count == tiles:
        every, order = by_heads(img_qkv, txt_kv, text_limit, tile_cols)
        attended = jnp.transpose(every, (1, 0, 2)).reshape(own_rows, all_heads * HD)
        w_attn_out = jnp.concatenate([w_attn_out[h * HD : (h + 1) * HD] for h in order], axis=0)
    else:
        img_block = img_qkv[0].reshape(tile_rows, grid_cols, 3, local_heads, HD)
        txt_block = txt_kv[0].reshape(1, text_rows, 2, local_heads, HD)
        img_mixed, txt_mixed = (
            lax.all_to_all(img_block, "col", split_axis=1, concat_axis=3, tiled=True),
            lax.all_to_all(txt_block, "col", split_axis=1, concat_axis=3, tiled=True),
        )
        img_flat = img_mixed.reshape(own_rows, 3, all_heads, HD)
        txt_flat = txt_mixed.reshape(text_rows // col_count, 2, all_heads, HD)
        key_value = jnp.concatenate([img_flat[:, 1:], txt_flat], axis=0)
        fold_step = make_fold(img_flat[:, 0], own_rows, text_rows // col_count, text_limit)
        carry = fold_step(
            start_carry(own_rows, all_heads),
            lax.all_gather(key_value, ("tile", "col"), axis=0, tiled=True),
            jnp.int32(0),
        )
        attended = finish(carry).reshape(own_rows, all_heads * HD)
    branch = jnp.dot(attended, w_attn_out, preferred_element_type=jnp.float32)
    step_now = step_index[0]
    mod_now = lax.dynamic_index_in_dim(modulation, step_now, 0, keepdims=False)[0]
    width = hidden_state.shape[3]
    mixed_state = (
        hidden_state[0].reshape(own_rows, width).astype(jnp.float32) + mod_now[0][None, :] * branch
    )
    row_mean = jnp.mean(mixed_state, axis=1, keepdims=True)
    centred = mixed_state - row_mean
    row_var = jnp.mean(centred * centred, axis=1, keepdims=True)
    normed = (
        centred / jnp.sqrt(row_var + norm_eps) * (1.0 + mod_now[2][None, :]) + mod_now[1][None, :]
    )
    normed = normed.astype(jnp.bfloat16)
    velocity = jnp.dot(normed, w_final, preferred_element_type=jnp.float32)
    channels = velocity.shape[1]
    sigma_step = sigmas[step_now + 1] - sigmas[step_now]
    updated = latent[0].reshape(own_rows, channels) + sigma_step * velocity
    grid_field = updated.reshape(tile_rows, tile_cols, channels)
    padded = padded_2(grid_field, (("tile", 0), ("col", 1)), 1)
    preview = jnp.zeros((tile_rows, tile_cols, channels), jnp.float32)
    for row_off in range(3):
        for col_off in range(3):
            preview = preview + jnp.einsum(
                "yxc,cd->yxd",
                padded[row_off : row_off + tile_rows, col_off : col_off + tile_cols],
                w_preview[row_off, col_off],
                precision=lax.Precision.HIGHEST,
            )
    return (velocity.reshape(1, tile_rows, tile_cols, channels), grid_field[None], preview[None])


def solution(mesh):
    placed = (
        P("req", "tile", None, None, "col"),
        P("req", "tile", None, "col"),
        P("req"),
        P("req", "tile", "col", None),
        P(None, "req", None, None),
        P(),
        P(),
        P("req", "tile", "col", None),
        P(),
        P(),
        P(),
    )
    return jax.shard_map(
        body,
        mesh=mesh,
        in_specs=placed,
        out_specs=(
            P("req", "tile", "col", None),
            P("req", "tile", "col", None),
            P("req", "tile", "col", None),
        ),
        check_vma=False,
    )
```

```python
import functools
import math

import jax
import jax.numpy as jnp
from jax import lax
from jax.experimental import pallas as pl
from jax.experimental.pallas import tpu as pltpu
from jax.sharding import PartitionSpec as P

HD = 128


norm_eps = 1e-06


def padded_2(cells, sides, width):
    for axis, dim in sides:
        count = lax.axis_size(axis)
        ends = count - 1
        head = lax.slice_in_dim(cells, 0, width, axis=dim)
        tail = lax.slice_in_dim(cells, cells.shape[dim] - width, cells.shape[dim], axis=dim)
        if count == 2:
            me = lax.axis_index(axis)
            came = lax.ppermute(jnp.where(me == 0, tail, head), axis, [(0, 1), (1, 0)])
            cells = jnp.concatenate(
                [jnp.where(me == 0, 0.0, came), cells, jnp.where(me == 0, came, 0.0)], axis=dim
            )
            continue
        cells = jnp.concatenate(
            [
                lax.ppermute(tail, axis, [(i, (i + 1) % count) for i in range(ends)]),
                cells,
                lax.ppermute(head, axis, [((i + 1) % count, i) for i in range(ends)]),
            ],
            axis=dim,
        )
    return cells


def make_fold(queries, img_rows, text_rows, text_limit):
    score_scale = 1.0 / math.sqrt(HD)
    shard_rows = img_rows + text_rows

    def fold_step(carry, piece, start):
        run_max, run_sum, run_acc = carry
        piece_len = piece.shape[0]
        key_index = jnp.arange(piece_len, dtype=jnp.int32)
        in_shard = key_index % shard_rows
        text_pos = key_index // shard_rows * text_rows + in_shard - img_rows
        key_live = (in_shard < img_rows) | (text_pos < text_limit)
        scores = (
            jnp.einsum("qhd,khd->hqk", queries, piece[:, 0], preferred_element_type=jnp.float32)
            * score_scale
        )
        scores = jnp.where(key_live[None, None, :], scores, -1e30)
        new_max = jnp.maximum(run_max, jnp.max(scores, axis=2))
        weights = jnp.where(key_live[None, None, :], jnp.exp(scores - new_max[:, :, None]), 0.0)
        run_sum = jnp.sum(weights, axis=2)
        run_acc = jnp.einsum(
            "hqk,khd->hqd",
            weights.astype(jnp.bfloat16),
            piece[:, 1],
            preferred_element_type=jnp.float32,
        )
        return (new_max, run_sum, run_acc)

    return fold_step


def start_carry(query_rows, head_count):
    return (
        jnp.full((head_count, query_rows), -1e30, jnp.float32),
        jnp.zeros((head_count, query_rows), jnp.float32),
        jnp.zeros((head_count, query_rows, HD), jnp.float32),
    )


def finish(carry):
    run_max, run_sum, run_acc = carry
    return jnp.transpose(run_acc / run_sum[:, :, None], (1, 0, 2)).astype(jnp.bfloat16)


def attend_kernel(moves, key_chunk, image_keys, q_ref, bias_ref, *refs):
    parts = refs[:-3]
    o_ref, kbuf, vbuf = refs[-3:]

    @pl.when(pl.program_id(0) == 0)
    def _():
        vbuf[:, HD:] = jnp.ones((vbuf.shape[0], HD), jnp.bfloat16)
        for which, block, k_from, v_from, size, to in moves:
            kbuf[to : to + size, :] = parts[which][block, k_from : k_from + size, :]
            vbuf[to : to + size, :HD] = parts[which][block, v_from : v_from + size, :]

    factor = math.log2(math.e) / math.sqrt(HD)
    queries = q_ref[0]
    all_keys = kbuf.shape[0]
    pieces = [(at, key_chunk) for at in range(0, image_keys, key_chunk)]
    pieces.append((image_keys, all_keys - image_keys))
    run_max = acc = None
    for at, size in pieces:
        scores = (
            lax.dot_general(
                queries,
                kbuf[at : at + size, :],
                (((1,), (1,)), ((), ())),
                preferred_element_type=jnp.float32,
            )
            * factor
        )
        if at == image_keys:
            scores = scores + bias_ref[...]
        top = jnp.max(scores, axis=1, keepdims=True)
        new_max = top if run_max is None else jnp.maximum(run_max, top)
        probs = jnp.exp2(scores - new_max).astype(jnp.bfloat16)
        term = jnp.dot(probs, vbuf[at : at + size, :], preferred_element_type=jnp.float32)
        acc = term if acc is None else acc * jnp.exp2(run_max - new_max) + term
        run_max = new_max
    o_ref[0] = (acc[:, :HD] / acc[:, HD:]).astype(jnp.bfloat16)


def attend(block, others, bias, query_rows, moves, image_keys, q_tile, key_chunk):
    blocks = block.shape[0]
    per_block = query_rows // q_tile
    all_keys = image_keys + bias.shape[1]
    parts = (block,) + others

    def whole(array):
        return pl.BlockSpec(array.shape, lambda i: (0,) * array.ndim)

    queries = blocks * query_rows
    return pl.pallas_call(
        functools.partial(attend_kernel, moves, key_chunk, image_keys),
        grid=(blocks * per_block,),
        out_shape=jax.ShapeDtypeStruct((blocks, query_rows, HD), jnp.bfloat16),
        in_specs=[
            pl.BlockSpec((1, q_tile, HD), lambda i: (i // per_block, i % per_block, 0)),
            whole(bias),
        ]
        + [whole(part) for part in parts],
        out_specs=pl.BlockSpec((1, q_tile, HD), lambda i: (i // per_block, i % per_block, 0)),
        scratch_shapes=[
            pltpu.VMEM((all_keys, HD), jnp.bfloat16),
            pltpu.VMEM((all_keys, 2 * HD), jnp.bfloat16),
        ],
        compiler_params=pltpu.CompilerParams(vmem_limit_bytes=48 * 1024 * 1024),
        cost_estimate=pl.CostEstimate(
            flops=6 * queries * all_keys * HD,
            bytes_accessed=2 * sum(part.size for part in parts) + 4 * queries * HD,
            transcendentals=queries * all_keys,
        ),
    )(block, bias, *parts)


def pack_whole_kernel(rows, halves, tile_cols, img_ref, txt_ref, o_ref):
    text_rows = txt_ref.shape[1]
    at = 0
    for part in range(3):
        for half in range(halves):
            for row in range(rows):
                start = (row * halves + half) * tile_cols
                o_ref[0, at : at + tile_cols, :] = img_ref[part, start : start + tile_cols, :]
                at += tile_cols
        if part:
            o_ref[0, at : at + text_rows, :] = txt_ref[part - 1]
            at += text_rows


def pack_halves_kernel(rows, halves, tile_cols, img_ref, txt_ref, o_ref):
    text_half = txt_ref.shape[1] // halves
    for half in range(halves):
        at = 0
        for part in range(3):
            for row in range(rows):
                start = (row * halves + half) * tile_cols
                o_ref[half, 0, at : at + tile_cols, :] = img_ref[
                    part, start : start + tile_cols, :
                ]
                at += tile_cols
            if part:
                o_ref[half, 0, at : at + text_half, :] = txt_ref[
                    part - 1, half * text_half : (half + 1) * text_half, :
                ]
                at += text_half


def pack_whole(img, txt, count, rows, halves, tile_cols):
    tokens, text_rows = img.shape[1], txt.shape[1]
    length = 3 * tokens + 2 * text_rows
    return pl.pallas_call(
        functools.partial(pack_whole_kernel, rows, halves, tile_cols),
        grid=(count,),
        out_shape=jax.ShapeDtypeStruct((count, length, HD), img.dtype),
        in_specs=[
            pl.BlockSpec((3, tokens, HD), lambda i: (0, 0, i)),
            pl.BlockSpec((2, text_rows, HD), lambda i: (0, 0, i)),
        ],
        out_specs=pl.BlockSpec((1, length, HD), lambda i: (i, 0, 0)),
        compiler_params=pltpu.CompilerParams(vmem_limit_bytes=32 * 1024 * 1024),
        cost_estimate=pl.CostEstimate(
            flops=0, bytes_accessed=4 * count * length * HD, transcendentals=0
        ),
    )(img, txt)


def pack_halves(img, txt, first, count, rows, halves, tile_cols):
    tokens, text_rows = img.shape[1], txt.shape[1]
    length = (3 * tokens + 2 * text_rows) // halves
    return pl.pallas_call(
        functools.partial(pack_halves_kernel, rows, halves, tile_cols),
        grid=(count,),
        out_shape=jax.ShapeDtypeStruct((halves, count, length, HD), img.dtype),
        in_specs=[
            pl.BlockSpec((3, tokens, HD), lambda i: (0, 0, first + i)),
            pl.BlockSpec((2, text_rows, HD), lambda i: (0, 0, first + i)),
        ],
        out_specs=pl.BlockSpec((halves, 1, length, HD), lambda i: (0, i, 0, 0)),
        compiler_params=pltpu.CompilerParams(vmem_limit_bytes=32 * 1024 * 1024),
        cost_estimate=pl.CostEstimate(
            flops=0, bytes_accessed=4 * halves * count * length * HD, transcendentals=0
        ),
    )(img, txt)


def tile_mixed(cells):
    return lax.all_to_all(cells, "tile", split_axis=0, concat_axis=0, tiled=True)


def tile_stepped(cells):
    count = lax.axis_size("tile")
    me = lax.axis_index("tile")
    held = []
    for step in range(count):
        block = lax.dynamic_index_in_dim(cells, (me + step) % count, 0, keepdims=True)
        if step:
            block = lax.ppermute(block, "tile", [(i, (i + step) % count) for i in range(count)])
        held.append(block)
    held = jnp.concatenate(held, axis=0)
    return jnp.concatenate(
        [
            lax.dynamic_index_in_dim(held, (me - source + count) % count, 0, keepdims=True)
            for source in range(count)
        ],
        axis=0,
    )


def col_swapped(cells, me, dim):
    kept = lax.dynamic_index_in_dim(cells, me, dim, keepdims=False)
    sent = lax.dynamic_index_in_dim(cells, 1 - me, dim, keepdims=False)
    came = lax.ppermute(sent, "col", [(0, 1), (1, 0)])
    return [jnp.where(me == 0, kept, came), jnp.where(me == 0, came, kept)]


def by_heads(img_qkv, txt_kv, text_limit, tile_cols):
    rows, grid_cols = img_qkv.shape[1:3]
    heads = img_qkv.shape[4] // HD
    text_rows = txt_kv.shape[1]
    tiles = lax.axis_size("tile")
    halves = grid_cols // tile_cols
    own = rows * tile_cols
    full = own * halves
    text_half = text_rows // halves
    me = lax.axis_index("col")

    img = jnp.transpose(img_qkv[0].reshape(full, 3, heads * HD), (1, 0, 2))
    txt = jnp.transpose(txt_kv[0], (1, 0, 2))
    send_a = pack_whole(img, txt, tiles, rows, halves, tile_cols)
    send_a, img, txt = lax.optimization_barrier((send_a, img, txt))
    got_a = tile_mixed(send_a)
    send_b = pack_halves(img, txt, tiles, heads - tiles, rows, halves, tile_cols)
    mixed_b = jnp.concatenate(col_swapped(send_b, me, 0), axis=0)
    mixed_b, got_a = lax.optimization_barrier((mixed_b, got_a))
    got_b = tile_mixed(mixed_b)

    text_all = tiles * text_rows
    image_all = tiles * full
    place = jnp.arange(text_all, dtype=jnp.int32)
    bias_a = jnp.where(place < text_limit, 0.0, -1e30).astype(jnp.float32)[None]
    side, within = place // (tiles * text_half), place % (tiles * text_half)
    place_b = (
        within // text_half * text_rows
        + jnp.where(side == 0, me, 1 - me) * text_half
        + within % text_half
    )
    bias_b = jnp.where(place_b < text_limit, 0.0, -1e30).astype(jnp.float32)[None]

    moves_a, moves_b = [], []
    for t in range(tiles):
        key, value = full, 2 * full + text_rows
        moves_a.append((0, t, key, value, full, t * full))
        moves_a.append((0, t, key + full, value + full, text_rows, image_all + t * text_rows))
    for s in range(halves):
        for t in range(tiles):
            key = own if s == 0 else 0
            value = key + own + text_half
            slot = s * tiles + t
            moves_b.append((s, t, key, value, own, slot * own))
            moves_b.append(
                (s, t, key + own, value + own, text_half, image_all + slot * text_half)
            )
    raw_a = attend(got_a, (), bias_a, full, tuple(moves_a), image_all, 512, 1024)
    raw_a, got_b = lax.optimization_barrier((raw_a, got_b))
    out_a = tile_mixed(raw_a)
    other_b = lax.ppermute(got_b[:, own:], "col", [(0, 1), (1, 0)])
    raw_b = attend(got_b, (other_b,), bias_b, own, tuple(moves_b), image_all, 512, 1024)
    out_b = tile_stepped(raw_b)
    out_a, raw_b = lax.optimization_barrier((out_a, raw_b))
    low, high = col_swapped(out_a.reshape(tiles, halves, own, HD), me, 1)
    third = heads - tiles
    every = jnp.concatenate([low, out_b[:third], high, out_b[third:]], axis=0)
    return jnp.transpose(every, (1, 0, 2)).reshape(own, halves * heads * HD)


def body(
    img_qkv,
    txt_kv,
    text_len,
    hidden_state,
    modulation,
    w_attn_out,
    w_final,
    latent,
    sigmas,
    step_index,
    w_preview,
):
    tile_rows = img_qkv.shape[1]
    grid_cols = img_qkv.shape[2]
    local_heads = img_qkv.shape[4] // HD
    text_rows = txt_kv.shape[1]
    tile_cols = hidden_state.shape[2]
    col_count = grid_cols // tile_cols
    own_rows = tile_rows * tile_cols
    text_limit = text_len[0]
    all_heads = local_heads * col_count
    tiles = lax.axis_size("tile")
    if col_count == 2 and (local_heads - tiles) * col_count == tiles:
        attended = by_heads(img_qkv, txt_kv, text_limit, tile_cols)
    else:
        img_block = img_qkv[0].reshape(tile_rows, grid_cols, 3, local_heads, HD)
        txt_block = txt_kv[0].reshape(1, text_rows, 2, local_heads, HD)
        img_mixed, txt_mixed = (
            lax.all_to_all(img_block, "col", split_axis=1, concat_axis=3, tiled=True),
            lax.all_to_all(txt_block, "col", split_axis=1, concat_axis=3, tiled=True),
        )
        img_flat = img_mixed.reshape(own_rows, 3, all_heads, HD)
        txt_flat = txt_mixed.reshape(text_rows // col_count, 2, all_heads, HD)
        key_value = jnp.concatenate([img_flat[:, 1:], txt_flat], axis=0)
        fold_step = make_fold(img_flat[:, 0], own_rows, text_rows // col_count, text_limit)
        carry = fold_step(
            start_carry(own_rows, all_heads),
            lax.all_gather(key_value, ("tile", "col"), axis=0, tiled=True),
            jnp.int32(0),
        )
        attended = finish(carry).reshape(own_rows, all_heads * HD)
    branch = jnp.dot(attended, w_attn_out, preferred_element_type=jnp.float32)
    step_now = step_index[0]
    mod_now = lax.dynamic_index_in_dim(modulation, step_now, 0, keepdims=False)[0]
    width = hidden_state.shape[3]
    mixed_state = (
        hidden_state[0].reshape(own_rows, width).astype(jnp.float32) + mod_now[0][None, :] * branch
    )
    row_mean = jnp.mean(mixed_state, axis=1, keepdims=True)
    centred = mixed_state - row_mean
    row_var = jnp.mean(centred * centred, axis=1, keepdims=True)
    normed = (
        centred / jnp.sqrt(row_var + norm_eps) * (1.0 + mod_now[2][None, :]) + mod_now[1][None, :]
    )
    normed = normed.astype(jnp.bfloat16)
    velocity = jnp.dot(normed, w_final, preferred_element_type=jnp.float32)
    channels = velocity.shape[1]
    sigma_step = sigmas[step_now + 1] - sigmas[step_now]
    updated = latent[0].reshape(own_rows, channels) + sigma_step * velocity
    grid_field = updated.reshape(tile_rows, tile_cols, channels)
    padded = padded_2(grid_field, (("col", 1), ("tile", 0)), 1)
    preview = jnp.zeros((tile_rows, tile_cols, channels), jnp.float32)
    for row_off in range(3):
        for col_off in range(3):
            preview = preview + jnp.einsum(
                "yxc,cd->yxd",
                padded[row_off : row_off + tile_rows, col_off : col_off + tile_cols],
                w_preview[row_off, col_off],
                precision=lax.Precision.HIGHEST,
            )
    return (velocity.reshape(1, tile_rows, tile_cols, channels), grid_field[None], preview[None])


def solution(mesh):
    placed = (
        P("req", "tile", None, None, "col"),
        P("req", "tile", None, "col"),
        P("req"),
        P("req", "tile", "col", None),
        P(None, "req", None, None),
        P(),
        P(),
        P("req", "tile", "col", None),
        P(),
        P(),
        P(),
    )
    return jax.shard_map(
        body,
        mesh=mesh,
        in_specs=placed,
        out_specs=(
            P("req", "tile", "col", None),
            P("req", "tile", "col", None),
            P("req", "tile", "col", None),
        ),
        check_vma=False,
    )
```

```python
import functools
import math

import jax
import jax.numpy as jnp
from jax import lax
from jax.experimental import pallas as pl
from jax.experimental.pallas import tpu as pltpu
from jax.sharding import PartitionSpec as P

HD = 128


norm_eps = 1e-06


def padded_2(cells, sides, width):
    for axis, dim in sides:
        count = lax.axis_size(axis)
        ends = count - 1
        head = lax.slice_in_dim(cells, 0, width, axis=dim)
        tail = lax.slice_in_dim(cells, cells.shape[dim] - width, cells.shape[dim], axis=dim)
        if count == 2:
            me = lax.axis_index(axis)
            came = lax.ppermute(jnp.where(me == 0, tail, head), axis, [(0, 1), (1, 0)])
            cells = jnp.concatenate(
                [jnp.where(me == 0, 0.0, came), cells, jnp.where(me == 0, came, 0.0)], axis=dim
            )
            continue
        cells = jnp.concatenate(
            [
                lax.ppermute(tail, axis, [(i, (i + 1) % count) for i in range(ends)]),
                cells,
                lax.ppermute(head, axis, [((i + 1) % count, i) for i in range(ends)]),
            ],
            axis=dim,
        )
    return cells


def make_fold(queries, img_rows, text_rows, text_limit):
    score_scale = 1.0 / math.sqrt(HD)
    shard_rows = img_rows + text_rows

    def fold_step(carry, piece, start):
        run_max, run_sum, run_acc = carry
        piece_len = piece.shape[0]
        key_index = jnp.arange(piece_len, dtype=jnp.int32)
        in_shard = key_index % shard_rows
        text_pos = key_index // shard_rows * text_rows + in_shard - img_rows
        key_live = (in_shard < img_rows) | (text_pos < text_limit)
        scores = (
            jnp.einsum("qhd,khd->hqk", queries, piece[:, 0], preferred_element_type=jnp.float32)
            * score_scale
        )
        scores = jnp.where(key_live[None, None, :], scores, -1e30)
        new_max = jnp.maximum(run_max, jnp.max(scores, axis=2))
        weights = jnp.where(key_live[None, None, :], jnp.exp(scores - new_max[:, :, None]), 0.0)
        run_sum = jnp.sum(weights, axis=2)
        run_acc = jnp.einsum(
            "hqk,khd->hqd",
            weights.astype(jnp.bfloat16),
            piece[:, 1],
            preferred_element_type=jnp.float32,
        )
        return (new_max, run_sum, run_acc)

    return fold_step


def start_carry(query_rows, head_count):
    return (
        jnp.full((head_count, query_rows), -1e30, jnp.float32),
        jnp.zeros((head_count, query_rows), jnp.float32),
        jnp.zeros((head_count, query_rows, HD), jnp.float32),
    )


def finish(carry):
    run_max, run_sum, run_acc = carry
    return jnp.transpose(run_acc / run_sum[:, :, None], (1, 0, 2)).astype(jnp.bfloat16)


def attend_kernel(moves, key_chunk, image_keys, q_ref, bias_ref, *refs):
    parts = refs[:-3]
    o_ref, kbuf, vbuf = refs[-3:]

    @pl.when(pl.program_id(0) == 0)
    def _():
        vbuf[:, HD:] = jnp.ones((vbuf.shape[0], HD), jnp.bfloat16)
        for which, block, k_from, v_from, size, to in moves:
            kbuf[to : to + size, :] = parts[which][block, k_from : k_from + size, :]
            vbuf[to : to + size, :HD] = parts[which][block, v_from : v_from + size, :]

    factor = math.log2(math.e) / math.sqrt(HD)
    queries = q_ref[0]
    all_keys = kbuf.shape[0]
    pieces = [(at, key_chunk) for at in range(0, image_keys, key_chunk)]
    pieces.append((image_keys, all_keys - image_keys))
    run_max = acc = None
    for at, size in pieces:
        scores = (
            lax.dot_general(
                queries,
                kbuf[at : at + size, :],
                (((1,), (1,)), ((), ())),
                preferred_element_type=jnp.float32,
            )
            * factor
        )
        if at == image_keys:
            scores = scores + bias_ref[...]
        top = jnp.max(scores, axis=1, keepdims=True)
        new_max = top if run_max is None else jnp.maximum(run_max, top)
        probs = jnp.exp2(scores - new_max).astype(jnp.bfloat16)
        term = jnp.dot(probs, vbuf[at : at + size, :], preferred_element_type=jnp.float32)
        acc = term if acc is None else acc * jnp.exp2(run_max - new_max) + term
        run_max = new_max
    o_ref[0] = (acc[:, :HD] / acc[:, HD:]).astype(jnp.bfloat16)


def attend(block, others, bias, query_rows, moves, image_keys, q_tile, key_chunk):
    blocks = block.shape[0]
    per_block = query_rows // q_tile
    all_keys = image_keys + bias.shape[1]
    parts = (block,) + others

    def whole(array):
        return pl.BlockSpec(array.shape, lambda i: (0,) * array.ndim)

    queries = blocks * query_rows
    return pl.pallas_call(
        functools.partial(attend_kernel, moves, key_chunk, image_keys),
        grid=(blocks * per_block,),
        out_shape=jax.ShapeDtypeStruct((blocks, query_rows, HD), jnp.bfloat16),
        in_specs=[
            pl.BlockSpec((1, q_tile, HD), lambda i: (i // per_block, i % per_block, 0)),
            whole(bias),
        ]
        + [whole(part) for part in parts],
        out_specs=pl.BlockSpec((1, q_tile, HD), lambda i: (i // per_block, i % per_block, 0)),
        scratch_shapes=[
            pltpu.VMEM((all_keys, HD), jnp.bfloat16),
            pltpu.VMEM((all_keys, 2 * HD), jnp.bfloat16),
        ],
        compiler_params=pltpu.CompilerParams(vmem_limit_bytes=48 * 1024 * 1024),
        cost_estimate=pl.CostEstimate(
            flops=6 * queries * all_keys * HD,
            bytes_accessed=2 * sum(part.size for part in parts) + 4 * queries * HD,
            transcendentals=queries * all_keys,
        ),
    )(block, bias, *parts)


def pack_whole_kernel(rows, halves, tile_cols, img_ref, txt_ref, o_ref):
    text_rows = txt_ref.shape[1]
    at = 0
    for part in range(3):
        for half in range(halves):
            for row in range(rows):
                start = (row * halves + half) * tile_cols
                o_ref[0, at : at + tile_cols, :] = img_ref[part, start : start + tile_cols, :]
                at += tile_cols
        if part:
            o_ref[0, at : at + text_rows, :] = txt_ref[part - 1]
            at += text_rows


def pack_halves_kernel(rows, halves, tile_cols, img_ref, txt_ref, o_ref):
    text_half = txt_ref.shape[1] // halves
    for half in range(halves):
        at = 0
        for part in range(3):
            for row in range(rows):
                start = (row * halves + half) * tile_cols
                o_ref[half, 0, at : at + tile_cols, :] = img_ref[
                    part, start : start + tile_cols, :
                ]
                at += tile_cols
            if part:
                o_ref[half, 0, at : at + text_half, :] = txt_ref[
                    part - 1, half * text_half : (half + 1) * text_half, :
                ]
                at += text_half


def pack_kernel(count, *args):
    img_ref, txt_ref, whole_ref, halves_ref = args[-4:]

    @pl.when(pl.program_id(0) < count)
    def _():
        pack_whole_kernel(*args[:-4], img_ref, txt_ref, whole_ref)

    @pl.when(pl.program_id(0) >= count)
    def _():
        pack_halves_kernel(*args[:-4], img_ref, txt_ref, halves_ref)


def pack(img, txt, count, heads, rows, halves, tile_cols):
    tokens, text_rows = img.shape[1], txt.shape[1]
    length = 3 * tokens + 2 * text_rows
    return pl.pallas_call(
        functools.partial(pack_kernel, count, rows, halves, tile_cols),
        grid=(heads,),
        out_shape=(
            jax.ShapeDtypeStruct((count, length, HD), img.dtype),
            jax.ShapeDtypeStruct((halves, heads - count, length // halves, HD), img.dtype),
        ),
        in_specs=[
            pl.BlockSpec((3, tokens, HD), lambda i: (0, 0, i)),
            pl.BlockSpec((2, text_rows, HD), lambda i: (0, 0, i)),
        ],
        out_specs=(
            pl.BlockSpec((1, length, HD), lambda i: (jnp.minimum(i, count - 1), 0, 0)),
            pl.BlockSpec(
                (halves, 1, length // halves, HD), lambda i: (0, jnp.maximum(i - count, 0), 0, 0)
            ),
        ),
        compiler_params=pltpu.CompilerParams(vmem_limit_bytes=32 * 1024 * 1024),
        cost_estimate=pl.CostEstimate(
            flops=0, bytes_accessed=4 * heads * length * HD, transcendentals=0
        ),
    )(img, txt)


def tile_mixed(cells):
    return lax.all_to_all(cells, "tile", split_axis=0, concat_axis=0, tiled=True)


def tile_stepped(cells):
    count = lax.axis_size("tile")
    me = lax.axis_index("tile")
    held = []
    for step in range(count):
        block = lax.dynamic_index_in_dim(cells, (me + step) % count, 0, keepdims=True)
        if step:
            block = lax.ppermute(block, "tile", [(i, (i + step) % count) for i in range(count)])
        held.append(block)
    held = jnp.concatenate(held, axis=0)
    return jnp.concatenate(
        [
            lax.dynamic_index_in_dim(held, (me - source + count) % count, 0, keepdims=True)
            for source in range(count)
        ],
        axis=0,
    )


def col_swapped(cells, me, dim):
    kept = lax.dynamic_index_in_dim(cells, me, dim, keepdims=False)
    sent = lax.dynamic_index_in_dim(cells, 1 - me, dim, keepdims=False)
    came = lax.ppermute(sent, "col", [(0, 1), (1, 0)])
    return [jnp.where(me == 0, kept, came), jnp.where(me == 0, came, kept)]


def by_heads(img_qkv, txt_kv, text_limit, tile_cols):
    rows, grid_cols = img_qkv.shape[1:3]
    heads = img_qkv.shape[4] // HD
    text_rows = txt_kv.shape[1]
    tiles = lax.axis_size("tile")
    halves = grid_cols // tile_cols
    own = rows * tile_cols
    full = own * halves
    text_half = text_rows // halves
    me = lax.axis_index("col")

    img = jnp.transpose(img_qkv[0].reshape(full, 3, heads * HD), (1, 0, 2))
    txt = jnp.transpose(txt_kv[0], (1, 0, 2))
    send_a, send_b = pack(img, txt, tiles, heads, rows, halves, tile_cols)
    got_a = tile_mixed(send_a)
    mixed_b = jnp.concatenate(col_swapped(send_b, me, 0), axis=0)
    mixed_b, got_a = lax.optimization_barrier((mixed_b, got_a))
    got_b = tile_mixed(mixed_b)

    text_all = tiles * text_rows
    image_all = tiles * full
    place = jnp.arange(text_all, dtype=jnp.int32)
    bias_a = jnp.where(place < text_limit, 0.0, -1e30).astype(jnp.float32)[None]
    side, within = place // (tiles * text_half), place % (tiles * text_half)
    place_b = (
        within // text_half * text_rows
        + jnp.where(side == 0, me, 1 - me) * text_half
        + within % text_half
    )
    bias_b = jnp.where(place_b < text_limit, 0.0, -1e30).astype(jnp.float32)[None]

    moves_a, moves_b = [], []
    for t in range(tiles):
        key, value = full, 2 * full + text_rows
        moves_a.append((0, t, key, value, full, t * full))
        moves_a.append((0, t, key + full, value + full, text_rows, image_all + t * text_rows))
    for s in range(halves):
        for t in range(tiles):
            key = own
            value = key + own + text_half
            slot = s * tiles + t
            moves_b.append((s, t, key, value, own, slot * own))
            moves_b.append(
                (s, t, key + own, value + own, text_half, image_all + slot * text_half)
            )
    raw_a = attend(got_a, (), bias_a, full, tuple(moves_a), image_all, 512, 1024)
    raw_a, got_b = lax.optimization_barrier((raw_a, got_b))
    out_a = lax.all_to_all(
        raw_a.reshape(tiles * halves, own, HD),
        ("tile", "col"),
        split_axis=0,
        concat_axis=0,
        tiled=True,
    ).reshape(tiles, halves, own, HD)
    other_b = lax.ppermute(got_b, "col", [(0, 1), (1, 0)])
    raw_b = attend(got_b, (other_b,), bias_b, own, tuple(moves_b), image_all, 512, 1024)
    out_b = tile_stepped(raw_b)
    out_a, raw_b = lax.optimization_barrier((out_a, raw_b))
    third = heads - tiles
    every = jnp.concatenate([out_a[:, 0], out_b[:third], out_a[:, 1], out_b[third:]], axis=0)
    return jnp.transpose(every, (1, 0, 2)).reshape(own, halves * heads * HD)


def body(
    img_qkv,
    txt_kv,
    text_len,
    hidden_state,
    modulation,
    w_attn_out,
    w_final,
    latent,
    sigmas,
    step_index,
    w_preview,
):
    tile_rows = img_qkv.shape[1]
    grid_cols = img_qkv.shape[2]
    local_heads = img_qkv.shape[4] // HD
    text_rows = txt_kv.shape[1]
    tile_cols = hidden_state.shape[2]
    col_count = grid_cols // tile_cols
    own_rows = tile_rows * tile_cols
    text_limit = text_len[0]
    all_heads = local_heads * col_count
    tiles = lax.axis_size("tile")
    if col_count == 2 and (local_heads - tiles) * col_count == tiles:
        attended = by_heads(img_qkv, txt_kv, text_limit, tile_cols)
    else:
        img_block = img_qkv[0].reshape(tile_rows, grid_cols, 3, local_heads, HD)
        txt_block = txt_kv[0].reshape(1, text_rows, 2, local_heads, HD)
        img_mixed, txt_mixed = (
            lax.all_to_all(img_block, "col", split_axis=1, concat_axis=3, tiled=True),
            lax.all_to_all(txt_block, "col", split_axis=1, concat_axis=3, tiled=True),
        )
        img_flat = img_mixed.reshape(own_rows, 3, all_heads, HD)
        txt_flat = txt_mixed.reshape(text_rows // col_count, 2, all_heads, HD)
        key_value = jnp.concatenate([img_flat[:, 1:], txt_flat], axis=0)
        fold_step = make_fold(img_flat[:, 0], own_rows, text_rows // col_count, text_limit)
        carry = fold_step(
            start_carry(own_rows, all_heads),
            lax.all_gather(key_value, ("tile", "col"), axis=0, tiled=True),
            jnp.int32(0),
        )
        attended = finish(carry).reshape(own_rows, all_heads * HD)
    branch = jnp.dot(attended, w_attn_out, preferred_element_type=jnp.float32)
    step_now = step_index[0]
    mod_now = lax.dynamic_index_in_dim(modulation, step_now, 0, keepdims=False)[0]
    width = hidden_state.shape[3]
    mixed_state = (
        hidden_state[0].reshape(own_rows, width).astype(jnp.float32) + mod_now[0][None, :] * branch
    )
    row_mean = jnp.mean(mixed_state, axis=1, keepdims=True)
    centred = mixed_state - row_mean
    row_var = jnp.mean(centred * centred, axis=1, keepdims=True)
    normed = (
        centred / jnp.sqrt(row_var + norm_eps) * (1.0 + mod_now[2][None, :]) + mod_now[1][None, :]
    )
    normed = normed.astype(jnp.bfloat16)
    velocity = jnp.dot(normed, w_final, preferred_element_type=jnp.float32)
    channels = velocity.shape[1]
    sigma_step = sigmas[step_now + 1] - sigmas[step_now]
    updated = latent[0].reshape(own_rows, channels) + sigma_step * velocity
    grid_field = updated.reshape(tile_rows, tile_cols, channels)
    padded = padded_2(grid_field, (("col", 1), ("tile", 0)), 1)
    preview = jnp.zeros((tile_rows, tile_cols, channels), jnp.float32)
    for row_off in range(3):
        for col_off in range(3):
            preview = preview + jnp.einsum(
                "yxc,cd->yxd",
                padded[row_off : row_off + tile_rows, col_off : col_off + tile_cols],
                w_preview[row_off, col_off],
                precision=lax.Precision.HIGHEST,
            )
    return (velocity.reshape(1, tile_rows, tile_cols, channels), grid_field[None], preview[None])


def solution(mesh):
    placed = (
        P("req", "tile", None, None, "col"),
        P("req", "tile", None, "col"),
        P("req"),
        P("req", "tile", "col", None),
        P(None, "req", None, None),
        P(),
        P(),
        P("req", "tile", "col", None),
        P(),
        P(),
        P(),
    )
    return jax.shard_map(
        body,
        mesh=mesh,
        in_specs=placed,
        out_specs=(
            P("req", "tile", "col", None),
            P("req", "tile", "col", None),
            P("req", "tile", "col", None),
        ),
        check_vma=False,
    )
```
